512 devices in a mesh: dp: 64 (over x, z, core), tensor: 8 (over y).
Axes of the slice: x: 4, y: 8, z: 8, core: 2. Of those that a mesh axis runs over, the one named last changes fastest.
Arguments:
- queries: bfloat16 [28672, 6144], P('dp', 'tensor'), may hold values from -6 to 6
- keys_in: bfloat16 [28672, 6144], P('dp', 'tensor'), may hold values from -6 to 6
- values: bfloat16 [28672, 6144], P('dp', 'tensor'), may hold values from -6 to 6
- q_gain: float32 [128], replicated, may hold values from 0.5 to 6
- k_gain: float32 [128], replicated, may hold values from 0.5 to 6
- cotangent: bfloat16 [16384, 6144], P(('dp', 'tensor')), may hold values from -6 to 6
- patch_counts: int32 [64, 6], replicated, may hold values from 0 to 240, as said below
- image_owner: int32 [64, 6], replicated, may hold values from 0 to 63, as said below
- pack_offset: int32 [64, 6], replicated, may hold values from 0 to 256, as said below
Outputs:
- attn_out: bfloat16 [16384, 6144], P(('dp', 'tensor'))
- grad_q: bfloat16 [28672, 6144], P('dp', 'tensor')
- grad_k: bfloat16 [28672, 6144], P('dp', 'tensor')
- grad_v: bfloat16 [28672, 6144], P('dp', 'tensor')
The draws below stay inside these ranges and needn't reach their ends.
Inputs may be any that keep to these rules, and one draw needn't show every extreme that they name: `patch_counts`: counts are multiples of 16; 0 marks an empty entry. The counts of one device sum to at most 448, reached on some device in every draw; the largest single image is reached in every draw. `image_owner`: an image's owner is the device itself or one of its two neighbours on the cycle (dp index plus or minus one modulo 64); of each device's 6 entries two stay, two go to each neighbour. The images that one device sends to one neighbour hold at most 96 patches in all, reached in every draw. `pack_offset`: the nonempty images owned by a device tile its 256 rows exactly.
All inputs are finite; a program needn't handle non-finite values.
Results may differ from the reference program's by a relative error of at most 0.029.
The reference program's roundings to bfloat16 on the way (of `query_norm`, `key_norm`, `weights_low` and `grad_scores`) count: a program that leaves them out, or rounds other values in their place, can miss the bound.
Values may be sent and summed in bfloat16 or wider, within the bound.
A program may use at most 64 MiB of HBM per device.

```python
import jax
import jax.numpy as jnp
from jax import lax

HEADS = 48
HD = 128
OWN_ROWS = 256
CAP = 96
SRC_ROWS = 448
OWN_TOKENS = 16384
SRC_TOKENS = 28672
N_DP = 64


def routing(key):
    cycle_size = N_DP
    blocks = CAP // 16
    streams = jax.random.split(key, 8)
    index = jnp.arange(cycle_size, dtype=jnp.int32)
    to_left = 16 * jax.random.randint(streams[0], (cycle_size,), 0, blocks + 1)
    to_right = 16 * jax.random.randint(streams[1], (cycle_size,), 0, blocks + 1)
    heavy = jax.random.randint(streams[2], (), 0, cycle_size)
    to_left = jnp.where(index == heavy, CAP, to_left)
    to_right = jnp.where(index == heavy, CAP, to_right)
    to_right = jnp.where(index == (heavy - 1) % cycle_size, 0, to_right)
    to_left = jnp.where(index == (heavy + 1) % cycle_size, 0, to_left)
    kept = OWN_ROWS - jnp.roll(to_right, 1) - jnp.roll(to_left, -1)
    left_part = 16 * jax.random.randint(streams[3], (cycle_size,), 0, to_left // 16 + 1)
    right_part = 16 * jax.random.randint(streams[4], (cycle_size,), 0, to_right // 16 + 1)
    kept_part = 16 * jax.random.randint(streams[5], (cycle_size,), 1, kept // 16)
    kept_part = jnp.where(index == heavy, kept - 16, kept_part)
    lengths = jnp.stack([left_part, to_left - left_part, kept_part, kept - kept_part, right_part, to_right - right_part], axis=1)
    owners = jnp.stack([index - 1, index - 1, index, index, index + 1, index + 1], axis=1) % cycle_size
    arrival = jnp.concatenate([jnp.roll(lengths[:, 4:6], 1, axis=0), lengths[:, 2:4], jnp.roll(lengths[:, 0:2], -1, axis=0)], axis=1)
    order = jax.vmap(lambda part_key: jax.random.permutation(part_key, 6))(jax.random.split(streams[6], cycle_size))
    placed = jnp.take_along_axis(arrival, order, axis=1)
    begins = jnp.cumsum(placed, axis=1) - placed
    inverse = jnp.argsort(order, axis=1)
    slot_begin = jnp.take_along_axis(begins, inverse, axis=1)
    offsets = jnp.concatenate([jnp.roll(slot_begin[:, 4:6], 1, axis=0), slot_begin[:, 2:4], jnp.roll(slot_begin[:, 0:2], -1, axis=0)], axis=1)
    shuffle = jax.vmap(lambda part_key: jax.random.permutation(part_key, 6))(jax.random.split(streams[7], cycle_size))
    counts = jnp.take_along_axis(lengths, shuffle, axis=1).astype(jnp.int32)
    owner_table = jnp.take_along_axis(owners, shuffle, axis=1).astype(jnp.int32)
    offset_table = jnp.take_along_axis(offsets, shuffle, axis=1).astype(jnp.int32)
    return (counts, owner_table, offset_table)


def draw_patch_counts(key, part):
    return routing(key)[0]


def draw_image_owner(key, part):
    return routing(key)[1]


def draw_pack_offset(key, part):
    return routing(key)[2]


def key_base(key):
    return jax.random.truncated_normal(key, -4.0, 4.0, (SRC_TOKENS, HEADS * HD), jnp.float32)


def draw_keys_in(key, part):
    base = key_base(key)
    return base.astype(jnp.bfloat16)


def draw_queries(key, part):
    base = key_base(key)
    key = jax.random.fold_in(key, 22)
    fresh = jax.random.truncated_normal(key, -4.0, 4.0, base.shape, jnp.float32)
    return fresh.astype(jnp.bfloat16)


def gain_values(key, low, high):
    return jnp.exp(jax.random.uniform(key, (HD,), jnp.float32, jnp.log(low), jnp.log(high)))


def draw_q_gain(key, part):
    key = jax.random.fold_in(key, 31)
    return gain_values(key, 0.7, 1.4)


def draw_k_gain(key, part):
    key = jax.random.fold_in(key, 32)
    return gain_values(key, 0.7, 1.4)


def level_of(stream_key, extent, cuts, least, high):
    level = 1.0
    for dim, parts in cuts:
        heights = jax.random.uniform(jax.random.fold_in(jax.random.fold_in(stream_key, 6), dim), (parts,), jnp.float32, least / len(cuts), high / len(cuts))
        level = level * jnp.repeat(jnp.exp(heights), extent[dim] // parts).reshape((-1,) + (1,) * (len(extent) - 1 - dim))
    return level


def normal_values(key, extent, spread, bound, shards=(), held_as=jnp.bfloat16):
    values = spread * jax.random.normal(key, extent, jnp.float32)
    if shards:
        values = values * level_of(key, extent, shards, -0.22, 0.18)
    return jnp.clip(values, -bound, bound).astype(held_as)


def setup_inputs(seed: int = 0) -> dict:
    key_list = jax.random.split(jax.random.key(seed), 10)
    return {
        "queries": draw_queries(jax.random.fold_in(key_list[9], 71), 0),
        "keys_in": draw_keys_in(jax.random.fold_in(key_list[9], 71), 0),
        "values": normal_values(key_list[2], (SRC_TOKENS, HEADS * HD), 1.0, 6.0, ((0, 64), (1, 8))),
        "q_gain": draw_q_gain(jax.random.fold_in(key_list[9], 71), 0),
        "k_gain": draw_k_gain(jax.random.fold_in(key_list[9], 71), 0),
        "cotangent": normal_values(key_list[5], (OWN_TOKENS, HEADS * HD), 1.0, 6.0, ((0, 512),)),
        "patch_counts": draw_patch_counts(jax.random.fold_in(key_list[9], 71), 0),
        "image_owner": draw_image_owner(jax.random.fold_in(key_list[9], 71), 0),
        "pack_offset": draw_pack_offset(jax.random.fold_in(key_list[9], 71), 0),
    }


EPS = 1e-06

def normalize(entries):
    centre = lax.optimization_barrier(jnp.mean(entries, axis=-1, keepdims=True))
    centred = entries - centre
    variance = lax.optimization_barrier(jnp.mean(centred * centred, axis=-1, keepdims=True))
    inverse = lax.rsqrt(variance + EPS)
    return (centred * inverse, inverse)

def norm_back(grad_norm, normed, inverse, gain):
    scaled = grad_norm * gain
    first = lax.optimization_barrier(jnp.mean(scaled, axis=-1, keepdims=True))
    second = lax.optimization_barrier(jnp.mean(scaled * normed, axis=-1, keepdims=True))
    return inverse * (scaled - first - normed * second)

def attend(queries, keys_in, values, cotangent, segment, q_gain, k_gain):
    row_count = queries.shape[0]
    head_size = q_gain.shape[0]
    head_count = queries.shape[1] // head_size
    shaped = (row_count, head_count, head_size)
    query_hat, query_inv = normalize(queries.reshape(shaped).astype(jnp.float32))
    key_hat, key_inv = normalize(keys_in.reshape(shaped).astype(jnp.float32))
    query_norm = (query_hat * q_gain).astype(jnp.bfloat16)
    key_norm = (key_hat * k_gain).astype(jnp.bfloat16)
    value_rows = values.reshape(shaped).astype(jnp.float32)
    cot_rows = cotangent.reshape(shaped).astype(jnp.float32)
    score_scale = head_size ** (-0.5)
    scores = jnp.einsum('qhd,khd->hqk', query_norm.astype(jnp.float32), key_norm.astype(jnp.float32)) * score_scale
    same_image = segment[:, None] == segment[None, :]
    scores = jnp.where(same_image[None], scores, -1e+30)
    row_max = lax.optimization_barrier(jnp.max(scores, axis=2, keepdims=True))
    powers = jnp.exp(scores - row_max)
    weights = powers / lax.optimization_barrier(jnp.sum(powers, axis=2, keepdims=True))
    weights_low = weights.astype(jnp.bfloat16)
    output = jnp.einsum('hqk,khd->qhd', weights_low.astype(jnp.float32), value_rows).astype(jnp.bfloat16)
    grad_weights = jnp.einsum('qhd,khd->hqk', cot_rows, value_rows)
    row_inner = lax.optimization_barrier(jnp.sum(weights * grad_weights, axis=2, keepdims=True))
    grad_scores = (weights * (grad_weights - row_inner) * score_scale).astype(jnp.bfloat16)
    grad_v = jnp.einsum('hqk,qhd->khd', weights_low.astype(jnp.float32), cot_rows).astype(jnp.bfloat16)
    grad_qnorm = jnp.einsum('hqk,khd->qhd', grad_scores.astype(jnp.float32), key_norm.astype(jnp.float32))
    grad_knorm = jnp.einsum('hqk,qhd->khd', grad_scores.astype(jnp.float32), query_norm.astype(jnp.float32))
    grad_q = norm_back(grad_qnorm, query_hat, query_inv, q_gain).astype(jnp.bfloat16)
    grad_k = norm_back(grad_knorm, key_hat, key_inv, k_gain).astype(jnp.bfloat16)
    flat_shape = (row_count, head_count * head_size)
    return (output.reshape(flat_shape), grad_q.reshape(flat_shape), grad_k.reshape(flat_shape), grad_v.reshape(flat_shape))

def reference(queries, keys_in, values, q_gain, k_gain, cotangent, patch_counts, image_owner, pack_offset):
    cycle_size = patch_counts.shape[0]
    entry_count = patch_counts.shape[1]
    total_own = cycle_size * OWN_ROWS
    starts = jnp.cumsum(patch_counts, axis=1) - patch_counts
    position = jnp.arange(SRC_ROWS, dtype=jnp.int32)[:, None]

    def place(source):
        begin_row = starts[source]
        counts = patch_counts[source]
        target = image_owner[source] * OWN_ROWS + pack_offset[source]
        labels = source * entry_count + jnp.arange(entry_count, dtype=jnp.int32)
        matches = (position >= begin_row[None]) & (position < (begin_row + counts)[None])
        in_use = jnp.any(matches, axis=1)
        within = position[:, 0] - lax.optimization_barrier(jnp.sum(jnp.where(matches, begin_row[None], 0), axis=1))
        target_row = lax.optimization_barrier(jnp.sum(jnp.where(matches, target[None], 0), axis=1)) + within
        label = lax.optimization_barrier(jnp.sum(jnp.where(matches, labels[None], 0), axis=1))
        return (jnp.where(in_use, target_row, total_own).astype(jnp.int32), label.astype(jnp.int32), in_use)
    target_row, label, in_use = jax.vmap(place)(jnp.arange(cycle_size, dtype=jnp.int32))
    target_row = target_row.reshape(-1)
    label = label.reshape(-1)
    in_use = in_use.reshape(-1)

    def to_owner(array):
        blank = jnp.zeros((total_own,) + array.shape[1:], array.dtype)
        return blank.at[target_row].set(array, mode='drop')
    packed_q = to_owner(queries).reshape(cycle_size, OWN_ROWS, -1)
    packed_k = to_owner(keys_in).reshape(cycle_size, OWN_ROWS, -1)
    packed_v = to_owner(values).reshape(cycle_size, OWN_ROWS, -1)
    segment = to_owner(label).reshape(cycle_size, OWN_ROWS)
    cot_packs = cotangent.reshape(cycle_size, OWN_ROWS, -1)

    def one_owner(pieces):
        return attend(pieces[0], pieces[1], pieces[2], pieces[3], pieces[4], q_gain, k_gain)
    owned_out, own_q, own_k, own_v = lax.map(one_owner, (packed_q, packed_k, packed_v, cot_packs, segment))
    attn_out = owned_out.reshape(total_own, -1)
    safe_row = jnp.minimum(target_row, total_own - 1)

    def to_source(array):
        gathered = array.reshape(total_own, -1)[safe_row]
        return jnp.where(in_use[:, None], gathered, jnp.zeros((), array.dtype))
    return (attn_out, to_source(own_q), to_source(own_k), to_source(own_v))
```

```python
import functools

import jax
import jax.numpy as jnp
from jax import lax
from jax.experimental import pallas as pl
from jax.experimental.pallas import tpu as pltpu
from jax.sharding import PartitionSpec as P

MESH = pl.DeviceIdType.MESH
HD = 128
OWN_ROWS = 256
CAP = 96
SRC_ROWS = 448
ENTRIES = 6
BLOCK = 16
TILES = 2
TILE = SRC_ROWS // TILES
OWN_BLOCKS = OWN_ROWS // BLOCK
CAP_BLOCKS = CAP // BLOCK
SRC_BLOCKS = SRC_ROWS // BLOCK
TILE_BLOCKS = TILE // BLOCK
EPS = 1e-06
BF16 = jnp.bfloat16
F32 = jnp.float32


def begins_of(counts, owners, wanted):
    begins, total = [], jnp.int32(0)
    chosen = [owner == wanted for owner in owners]
    for count, mine in zip(counts, chosen):
        begins.append(total)
        total = total + jnp.where(mine, count, 0)
    return chosen, begins


def slot_source(chosen, begins, targets, block):
    shift = jnp.int32(0)
    for mine, begin, target in zip(chosen, begins, targets):
        shift = jnp.where(mine & (block >= begin), target - begin, shift)
    return block + shift


def lane_mean(x):
    return jnp.sum(x, axis=-1, keepdims=True) * (1.0 / HD)


def normalize(x):
    centred = x - lane_mean(x)
    inverse = lax.rsqrt(lane_mean(centred * centred) + EPS)
    return centred * inverse, inverse


def norm_back(grad, normed, inverse, gain):
    scaled = grad * gain
    first = lane_mean(scaled)
    second = lane_mean(scaled * normed)
    return inverse * (scaled - first - normed * second)


def dot(a, b, dims):
    return lax.dot_general(a, b, (dims, ((), ())), preferred_element_type=F32)


def kernel(
    n_dp, n_t, heads,
    q_hbm, k_hbm, v_hbm, cot_hbm, qg_hbm, kg_hbm, cnt_hbm, own_hbm, off_hbm,
    attn, gq_out, gk_out, gv_out,
    q_in, k_in, v_in, qg, kg, cnt, own, off,
    qn, kn, qh, kh, qi, ki, w_s, bias,
    sout, cat, lsend, rsend, pack,
    cown, ccat, lret, rret, csrc,
    in_sem, tab_sem, local_sem, a_send, a_recv, b_send, b_recv, d_send, d_recv,
):
    me_d = lax.axis_index("dp")
    me_t = lax.axis_index("tensor")
    left = lax.rem(me_d + n_dp - 1, n_dp)
    right = lax.rem(me_d + 1, n_dp)
    width = heads * HD
    blocks_t = OWN_BLOCKS // n_t
    peers = [lax.rem(me_t + s, n_t) for s in range(1, n_t)]

    loads = [
        pltpu.make_async_copy(src, dst, in_sem.at[i])
        for i, (src, dst) in enumerate(
            [(q_hbm, q_in), (k_hbm, k_in), (v_hbm, v_in), (qg_hbm, qg), (kg_hbm, kg)]
        )
    ]
    tables = [
        pltpu.make_async_copy(src, dst, tab_sem.at[i])
        for i, (src, dst) in enumerate([(cnt_hbm, cnt), (own_hbm, own), (off_hbm, off)])
    ]
    for copy in tables + loads:
        copy.start()

    barrier = pltpu.get_barrier_semaphore()
    for peer in peers:
        pl.semaphore_signal(barrier, inc=1, device_id={"tensor": peer}, device_id_type=MESH)
    for peer in (left, right):
        pl.semaphore_signal(barrier, inc=1, device_id={"dp": peer}, device_id_type=MESH)
    pl.semaphore_wait(barrier, n_t + 1)

    def cols(index):
        return pl.ds(pl.multiple_of(index * width, width), width)

    def token_blocks(index):
        return pl.ds(index * blocks_t, blocks_t)

    cot_copies = [
        pltpu.make_async_remote_copy(
            src_ref=cot_hbm.at[:, :, cols(peer)], dst_ref=cown.at[token_blocks(me_t)],
            send_sem=a_send.at[i], recv_sem=a_recv.at[i],
            device_id={"tensor": peer}, device_id_type=MESH,
        )
        for i, peer in enumerate(peers)
    ]
    for copy in cot_copies:
        copy.start()
    cot_local = pltpu.make_async_copy(
        cot_hbm.at[:, :, cols(me_t)], cown.at[token_blocks(me_t)], local_sem.at[0]
    )
    cot_local.start()

    for copy in tables:
        copy.wait()

    def entries(source):
        counts = [cnt[j, source] >> 4 for j in range(ENTRIES)]
        owners = [own[j, source] for j in range(ENTRIES)]
        offsets = [off[j, source] >> 4 for j in range(ENTRIES)]
        return counts, owners, offsets

    counts, owners, offsets = entries(me_d)
    l_counts, l_owners, l_offsets = entries(left)
    r_counts, r_owners, r_offsets = entries(right)
    starts, ends, total = [], [], jnp.int32(0)
    for count in counts:
        starts.append(total)
        total = total + count
        ends.append(total)
    to_left, left_begins = begins_of(counts, owners, left)
    to_right, right_begins = begins_of(counts, owners, right)
    from_left, fl_begins = begins_of(l_counts, l_owners, me_d)
    from_right, fr_begins = begins_of(r_counts, r_owners, me_d)

    key_row = lax.broadcasted_iota(jnp.int32, (SRC_ROWS, 1), 0)
    key_seg = jnp.zeros((SRC_ROWS, 1), jnp.int32)
    for end in ends:
        key_seg = key_seg + (key_row >= end * BLOCK).astype(jnp.int32)
    for i in range(TILES):
        query_row = lax.broadcasted_iota(jnp.int32, (1, TILE), 1) + i * TILE
        query_seg = jnp.zeros((1, TILE), jnp.int32)
        for end in ends:
            query_seg = query_seg + (query_row >= end * BLOCK).astype(jnp.int32)
        bias[i] = jnp.where(key_seg == query_seg, 0.0, -1e30).astype(F32)

    for copy in loads:
        copy.wait()

    scale = HD ** -0.5

    def forward(h, carry):
        lanes = pl.ds(pl.multiple_of(h * HD, HD), HD)
        query_hat, query_inv = normalize(q_in[:, lanes].astype(F32))
        key_hat, key_inv = normalize(k_in[:, lanes].astype(F32))
        qh[h] = query_hat
        kh[h] = key_hat
        qi[h] = query_inv
        ki[h] = key_inv
        qn[h] = (query_hat * qg[...]).astype(BF16)
        kn[h] = (key_hat * kg[...]).astype(BF16)
        value = v_in[:, lanes]
        for i in range(TILES):
            rows = pl.ds(i * TILE, TILE)
            scores = dot(kn[h], qn[h, rows, :], ((1,), (1,))) * scale + bias[i]
            powers = jnp.exp(scores - jnp.max(scores, axis=0, keepdims=True))
            weights = powers * (1.0 / jnp.sum(powers, axis=0, keepdims=True))
            w_s[h, i] = weights
            out = dot(weights.astype(BF16), value, ((0,), (0,))).astype(BF16)
            out = out.reshape(TILE_BLOCKS, BLOCK, HD)
            blocks = pl.ds(i * TILE_BLOCKS, TILE_BLOCKS)
            sout[blocks, :, lanes] = out
            cat[blocks, :, lanes] = out
        return carry

    lax.fori_loop(0, heads, forward, 0)

    def gather(dst, block, src, index):
        dst[block] = src[jnp.clip(index, 0, src.shape[0] - 1)]

    for block in range(CAP_BLOCKS):
        gather(lsend, block, sout, slot_source(to_left, left_begins, starts, block))
        gather(rsend, block, sout, slot_source(to_right, right_begins, starts, block))

    def exchange(to_l, to_r, dst, base, first):
        return [
            pltpu.make_async_remote_copy(
                src_ref=to_l, dst_ref=dst.at[pl.ds(base + CAP_BLOCKS, CAP_BLOCKS)],
                send_sem=d_send.at[first], recv_sem=d_recv.at[first],
                device_id={"dp": left}, device_id_type=MESH,
            ),
            pltpu.make_async_remote_copy(
                src_ref=to_r, dst_ref=dst.at[pl.ds(base, CAP_BLOCKS)],
                send_sem=d_send.at[first + 1], recv_sem=d_recv.at[first + 1],
                device_id={"dp": right}, device_id_type=MESH,
            ),
        ]

    out_moves = exchange(lsend, rsend, cat, SRC_BLOCKS, 0)
    for copy in out_moves:
        copy.start()
    for copy in out_moves:
        copy.wait()

    for block in range(OWN_BLOCKS):
        shift = jnp.int32(0)
        for j in range(ENTRIES):
            for mine, base, offset, count in (
                (owners[j] == me_d, starts[j], offsets[j], counts[j]),
                (from_left[j], SRC_BLOCKS + fl_begins[j], l_offsets[j], l_counts[j]),
                (from_right[j], SRC_BLOCKS + CAP_BLOCKS + fr_begins[j], r_offsets[j], r_counts[j]),
            ):
                inside = mine & (offset <= block) & (block < offset + count)
                shift = jnp.where(inside, base - offset, shift)
        gather(pack, block, cat, block + shift)

    out_copies = [
        pltpu.make_async_remote_copy(
            src_ref=pack.at[token_blocks(peer)], dst_ref=attn.at[:, :, cols(me_t)],
            send_sem=b_send.at[i], recv_sem=b_recv.at[i],
            device_id={"tensor": peer}, device_id_type=MESH,
        )
        for i, peer in enumerate(peers)
    ]
    for copy in out_copies:
        copy.start()
    out_local = pltpu.make_async_copy(
        pack.at[token_blocks(me_t)], attn.at[:, :, cols(me_t)], local_sem.at[1]
    )
    out_local.start()

    cot_local.wait()
    for copy in cot_copies:
        copy.wait()
    for block in range(CAP_BLOCKS):
        gather(lret, block, cown, slot_source(from_left, fl_begins, l_offsets, block))
        gather(rret, block, cown, slot_source(from_right, fr_begins, r_offsets, block))
    cot_moves = exchange(lret, rret, ccat, OWN_BLOCKS, 2)
    for copy in cot_moves:
        copy.start()
    ccat[pl.ds(0, OWN_BLOCKS)] = cown[...]
    for copy in cot_moves:
        copy.wait()
    for block in range(SRC_BLOCKS):
        shift = jnp.int32(0)
        for j in range(ENTRIES):
            base = jnp.where(
                owners[j] == me_d,
                offsets[j],
                jnp.where(to_left[j], OWN_BLOCKS + left_begins[j], OWN_BLOCKS + CAP_BLOCKS + right_begins[j]),
            )
            shift = jnp.where(block >= starts[j], base - starts[j], shift)
        gather(csrc, block, ccat, block + shift)

    in_use = key_row < total * BLOCK

    def backward(h, carry):
        lanes = pl.ds(pl.multiple_of(h * HD, HD), HD)
        value = v_in[:, lanes]
        grad_v = jnp.zeros((SRC_ROWS, HD), F32)
        grad_k = jnp.zeros((SRC_ROWS, HD), F32)
        grad_q = []
        for i in range(TILES):
            rows = pl.ds(i * TILE, TILE)
            cot = csrc[pl.ds(i * TILE_BLOCKS, TILE_BLOCKS), :, lanes].reshape(TILE, HD)
            weights = w_s[h, i]
            grad_w = dot(value, cot, ((1,), (1,)))
            inner = jnp.sum(weights * grad_w, axis=0, keepdims=True)
            grad_s = (weights * (grad_w - inner) * scale).astype(BF16)
            grad_v = grad_v + dot(weights.astype(BF16), cot, ((1,), (0,)))
            grad_k = grad_k + dot(grad_s, qn[h, rows, :], ((1,), (0,)))
            grad_q.append(dot(grad_s, kn[h], ((0,), (0,))))
        grad_q = norm_back(jnp.concatenate(grad_q, axis=0), qh[h], qi[h], qg[...])
        grad_k = norm_back(grad_k, kh[h], ki[h], kg[...])
        gq_out[:, lanes] = jnp.where(in_use, grad_q, 0.0).astype(BF16)
        gk_out[:, lanes] = jnp.where(in_use, grad_k, 0.0).astype(BF16)
        gv_out[:, lanes] = jnp.where(in_use, grad_v, 0.0).astype(BF16)
        return carry

    lax.fori_loop(0, heads, backward, 0)

    out_local.wait()
    for copy in out_copies:
        copy.wait()


def store_kernel(a, b, c, d, a_out, b_out, c_out, d_out, sem):
    copies = [
        pltpu.make_async_copy(src, dst, sem.at[i])
        for i, (src, dst) in enumerate(((a, a_out), (b, b_out), (c, c_out), (d, d_out)))
    ]
    for copy in copies:
        copy.start()
    for copy in copies:
        copy.wait()


def per_device(queries, keys_in, values, q_gain, k_gain, cotangent, patch_counts, image_owner, pack_offset):
    n_dp, n_t = lax.axis_size("dp"), lax.axis_size("tensor")
    width = queries.shape[1]
    heads = width // HD
    grad_shape = queries.shape
    attn_shape = (cotangent.shape[0] // BLOCK, BLOCK, cotangent.shape[1])
    dma = pltpu.SemaphoreType.DMA
    vmem = pltpu.VMEM

    def blocks(count):
        return vmem((count, BLOCK, width), BF16)

    scratch = [
        vmem((SRC_ROWS, width), BF16), vmem((SRC_ROWS, width), BF16), vmem((SRC_ROWS, width), BF16),
        vmem((1, HD), F32), vmem((1, HD), F32),
        pltpu.SMEM((ENTRIES, n_dp), jnp.int32),
        pltpu.SMEM((ENTRIES, n_dp), jnp.int32),
        pltpu.SMEM((ENTRIES, n_dp), jnp.int32),
        vmem((heads, SRC_ROWS, HD), BF16), vmem((heads, SRC_ROWS, HD), BF16),
        vmem((heads, SRC_ROWS, HD), F32), vmem((heads, SRC_ROWS, HD), F32),
        vmem((heads, SRC_ROWS, 1), F32), vmem((heads, SRC_ROWS, 1), F32),
        vmem((heads, TILES, SRC_ROWS, TILE), F32),
        vmem((TILES, SRC_ROWS, TILE), F32),
        blocks(SRC_BLOCKS), blocks(SRC_BLOCKS + 2 * CAP_BLOCKS),
        blocks(CAP_BLOCKS), blocks(CAP_BLOCKS), blocks(OWN_BLOCKS),
        blocks(OWN_BLOCKS), blocks(OWN_BLOCKS + 2 * CAP_BLOCKS),
        blocks(CAP_BLOCKS), blocks(CAP_BLOCKS), blocks(SRC_BLOCKS),
        dma((5,)), dma((3,)), dma((2,)),
        dma((n_t - 1,)), dma((n_t - 1,)), dma((n_t - 1,)), dma((n_t - 1,)), dma((4,)), dma((4,)),
    ]
    any_spec = pl.BlockSpec(memory_space=pl.ANY)
    vmem_spec = pl.BlockSpec(memory_space=pltpu.VMEM)
    flops = 12 * heads * SRC_ROWS * SRC_ROWS * HD
    operands = (
        queries, keys_in, values, cotangent.reshape(attn_shape), q_gain.reshape(1, HD), k_gain.reshape(1, HD),
        patch_counts.T, image_owner.T, pack_offset.T,
    )
    held = pl.pallas_call(
        functools.partial(kernel, n_dp, n_t, heads),
        out_shape=[vmem(attn_shape, BF16)] + [vmem(grad_shape, BF16)] * 3,
        in_specs=[any_spec] * 9,
        out_specs=[vmem_spec] * 4,
        scratch_shapes=scratch,
        compiler_params=pltpu.CompilerParams(
            collective_id=0, has_side_effects=True, vmem_limit_bytes=40 * 2**20
        ),
        cost_estimate=pl.CostEstimate(flops=flops, bytes_accessed=5 * 2**20, transcendentals=0),
    )(*[pltpu.with_memory_space_constraint(x, pltpu.HBM) for x in operands])
    held = [pltpu.with_memory_space_constraint(x, pltpu.VMEM) for x in held]
    attn_out, grad_q, grad_k, grad_v = pl.pallas_call(
        store_kernel,
        out_shape=[jax.ShapeDtypeStruct(x.shape, BF16) for x in held],
        in_specs=[vmem_spec] * 4,
        out_specs=[any_spec] * 4,
        scratch_shapes=[dma((4,))],
        compiler_params=pltpu.CompilerParams(vmem_limit_bytes=16 * 2**20),
        cost_estimate=pl.CostEstimate(flops=0, bytes_accessed=5 * 2**20, transcendentals=0),
    )(*held)
    return attn_out.reshape(cotangent.shape), grad_q, grad_k, grad_v


def solution(mesh):
    in_specs = (
        P("dp", "tensor"),
        P("dp", "tensor"),
        P("dp", "tensor"),
        P(),
        P(),
        P(("dp", "tensor"), None),
        P(),
        P(),
        P(),
    )
    out_specs = (P(("dp", "tensor"), None), P("dp", "tensor"), P("dp", "tensor"), P("dp", "tensor"))
    return jax.shard_map(
        per_device, mesh=mesh, in_specs=in_specs, out_specs=out_specs, check_vma=False
    )
```

```python
import functools

import jax
import jax.numpy as jnp
from jax import lax
from jax.experimental import pallas as pl
from jax.experimental.pallas import tpu as pltpu
from jax.sharding import PartitionSpec as P

MESH = pl.DeviceIdType.MESH
HD = 128
OWN_ROWS = 256
CAP = 96
SRC_ROWS = 448
ENTRIES = 6
BLOCK = 16
OWN_BLOCKS = OWN_ROWS // BLOCK
CAP_BLOCKS = CAP // BLOCK
SRC_BLOCKS = SRC_ROWS // BLOCK
CHUNKS = (3, 3)
LOG2E = 1.4426950408889634
EPS = 1e-06
BF16 = jnp.bfloat16
F32 = jnp.float32


def begins_of(counts, owners, wanted):
    begins, total = [], jnp.int32(0)
    chosen = [owner == wanted for owner in owners]
    for count, mine in zip(counts, chosen):
        begins.append(total)
        total = total + jnp.where(mine, count, 0)
    return chosen, begins


def slot_source(chosen, begins, targets, block):
    shift = jnp.int32(0)
    for mine, begin, target in zip(chosen, begins, targets):
        shift = jnp.where(mine & (block >= begin), target - begin, shift)
    return block + shift


def lane_mean(x):
    return jnp.sum(x, axis=-1, keepdims=True) * (1.0 / HD)


def normalize(x):
    centred = x - lane_mean(x)
    inverse = lax.rsqrt(lane_mean(centred * centred) + EPS)
    return centred * inverse, inverse


def norm_back(grad, normed, inverse, gain):
    scaled = grad * gain
    first = lane_mean(scaled)
    second = lane_mean(scaled * normed)
    return inverse * (scaled - first - normed * second)


def dot(a, b, dims):
    return lax.dot_general(a, b, (dims, ((), ())), preferred_element_type=F32)


def kernel(n_dp, n_t, heads, *refs):
    (q_hbm, k_hbm, v_hbm, cot_hbm, qg_hbm, kg_hbm, cnt_hbm, own_hbm, off_hbm) = refs[:9]
    attn, gq_out, gk_out, gv_out = refs[9:13]
    (q_in, k_in, v_in, qg, kg, cnt, own, off, qn, kn, qh, kh, qi, ki, w_s, bias) = refs[13:29]
    in_sem, tab_sem, local_sem, a_send, a_recv, b_send, b_recv, d_send, d_recv, ready = refs[29:39]
    parts = [refs[39 + 10 * c: 49 + 10 * c] for c in range(len(CHUNKS))]
    firsts = [sum(CHUNKS[:c]) for c in range(len(CHUNKS))]

    me_d = lax.axis_index("dp")
    me_t = lax.axis_index("tensor")
    left = lax.rem(me_d + n_dp - 1, n_dp)
    right = lax.rem(me_d + 1, n_dp)
    width = heads * HD
    blocks_t = OWN_BLOCKS // n_t
    steps = sorted(range(1, n_t), key=lambda s: (-min(s, n_t - s), s))
    peers = [lax.rem(me_t + s, n_t) for s in steps]

    tables = [
        pltpu.make_async_copy(src, dst, tab_sem.at[i])
        for i, (src, dst) in enumerate([(cnt_hbm, cnt), (own_hbm, own), (off_hbm, off)])
    ]
    loads = [
        pltpu.make_async_copy(src, dst, in_sem.at[i])
        for i, (src, dst) in enumerate(
            [(q_hbm, q_in), (k_hbm, k_in), (v_hbm, v_in), (qg_hbm, qg), (kg_hbm, kg)]
        )
    ]
    barrier = pltpu.get_barrier_semaphore()
    for peer in peers:
        pl.semaphore_signal(barrier, inc=1, device_id={"tensor": peer}, device_id_type=MESH)
    pl.semaphore_signal(barrier, inc=1, device_id={"dp": left}, device_id_type=MESH)
    for copy in tables + loads:
        copy.start()
    pl.semaphore_wait(barrier, n_t)
    pl.semaphore_signal(ready, inc=1, device_id={"dp": right}, device_id_type=MESH)

    def cols(index, c):
        return pl.ds(pl.multiple_of(index * width + firsts[c] * HD, HD), CHUNKS[c] * HD)

    def token_blocks(index):
        return pl.ds(index * blocks_t, blocks_t)

    cot_copies, out_copies, cot_local, out_local = [], [], [], []
    for c, part in enumerate(parts):
        pack, cown = part[4], part[5]
        cot_copies.append([
            pltpu.make_async_remote_copy(
                src_ref=cot_hbm.at[:, :, cols(peer, c)], dst_ref=cown.at[token_blocks(me_t)],
                send_sem=a_send.at[c, i], recv_sem=a_recv.at[c, i],
                device_id={"tensor": peer}, device_id_type=MESH,
            )
            for i, peer in enumerate(peers)
        ])
        cot_local.append(pltpu.make_async_copy(
            cot_hbm.at[:, :, cols(me_t, c)], cown.at[token_blocks(me_t)], local_sem.at[0, c]
        ))
        out_copies.append([
            pltpu.make_async_remote_copy(
                src_ref=pack.at[token_blocks(peer)], dst_ref=attn.at[:, :, cols(me_t, c)],
                send_sem=b_send.at[c, i], recv_sem=b_recv.at[c, i],
                device_id={"tensor": peer}, device_id_type=MESH,
            )
            for i, peer in enumerate(peers)
        ])
        out_local.append(pltpu.make_async_copy(
            pack.at[token_blocks(me_t)], attn.at[:, :, cols(me_t, c)], local_sem.at[1, c]
        ))
    for c in range(len(CHUNKS)):
        for copy in cot_copies[c]:
            copy.start()
        cot_local[c].start()

    for copy in tables:
        copy.wait()

    def entries(source):
        counts = [cnt[j, source] >> 4 for j in range(ENTRIES)]
        owners = [own[j, source] for j in range(ENTRIES)]
        offsets = [off[j, source] >> 4 for j in range(ENTRIES)]
        return counts, owners, offsets

    counts, owners, offsets = entries(me_d)
    l_counts, l_owners, l_offsets = entries(left)
    r_counts, r_owners, r_offsets = entries(right)
    starts, ends, total = [], [], jnp.int32(0)
    for count in counts:
        starts.append(total)
        total = total + count
        ends.append(total)
    to_left, left_begins = begins_of(counts, owners, left)
    to_right, right_begins = begins_of(counts, owners, right)
    from_left, fl_begins = begins_of(l_counts, l_owners, me_d)
    from_right, fr_begins = begins_of(r_counts, r_owners, me_d)

    def segments(axis):
        row = lax.broadcasted_iota(jnp.int32, (SRC_ROWS, 1) if axis == 0 else (1, SRC_ROWS), axis)
        segment = jnp.zeros(row.shape, jnp.int32)
        for end in ends:
            segment = segment + (row >= end * BLOCK).astype(jnp.int32)
        return segment

    bias[...] = jnp.where(segments(0) == segments(1), 0.0, -1e30).astype(F32)
    in_use = lax.broadcasted_iota(jnp.int32, (SRC_ROWS, 1), 0) < total * BLOCK

    for copy in loads:
        copy.wait()

    scale = HD ** -0.5

    def forward(c):
        sout, cat = parts[c][0], parts[c][1]
        for h in range(firsts[c], firsts[c] + CHUNKS[c]):
            lanes = pl.ds(h * HD, HD)
            query_hat, query_inv = normalize(q_in[:, lanes].astype(F32))
            key_hat, key_inv = normalize(k_in[:, lanes].astype(F32))
            qh[h] = query_hat
            kh[h] = key_hat
            qi[h] = jnp.broadcast_to(query_inv, (SRC_ROWS, HD))
            ki[h] = jnp.broadcast_to(key_inv, (SRC_ROWS, HD))
            query_norm = (query_hat * qg[...]).astype(BF16)
            key_norm = (key_hat * kg[...]).astype(BF16)
            qn[h] = query_norm
            kn[h] = key_norm
            scores = dot(key_norm, query_norm, ((1,), (1,))) + bias[...]
            powers = jnp.exp2((scores - jnp.max(scores, axis=0, keepdims=True)) * (scale * LOG2E))
            weights = powers * (1.0 / jnp.sum(powers, axis=0, keepdims=True))
            w_s[h] = weights
            out = dot(weights.astype(BF16), v_in[:, lanes], ((0,), (0,))).astype(BF16)
            out = out.reshape(SRC_BLOCKS, BLOCK, HD)
            local = pl.ds((h - firsts[c]) * HD, HD)
            sout[:, :, local] = out
            cat[pl.ds(0, SRC_BLOCKS), :, local] = out

    def backward(c):
        csrc = parts[c][9]
        for h in range(firsts[c], firsts[c] + CHUNKS[c]):
            lanes = pl.ds(h * HD, HD)
            cot = csrc[:, :, pl.ds((h - firsts[c]) * HD, HD)].reshape(SRC_ROWS, HD)
            weights = w_s[h]
            grad_w = dot(v_in[:, lanes], cot, ((1,), (1,)))
            inner = jnp.sum(weights * grad_w, axis=0, keepdims=True)
            grad_s = (weights * (grad_w - inner) * scale).astype(BF16)
            grad_v = dot(weights.astype(BF16), cot, ((1,), (0,)))
            grad_k = dot(grad_s, qn[h], ((1,), (0,)))
            grad_q = dot(grad_s, kn[h], ((0,), (0,)))
            grad_q = norm_back(grad_q, qh[h], qi[h], qg[...])
            grad_k = norm_back(grad_k, kh[h], ki[h], kg[...])
            gq_out[:, lanes] = jnp.where(in_use, grad_q, 0.0).astype(BF16)
            gk_out[:, lanes] = jnp.where(in_use, grad_k, 0.0).astype(BF16)
            gv_out[:, lanes] = jnp.where(in_use, grad_v, 0.0).astype(BF16)

    def gather(dst, block, src, index):
        dst[block] = src[jnp.clip(index, 0, src.shape[0] - 1)]

    def exchange(to_l, to_r, dst, base, first, c):
        return [
            pltpu.make_async_remote_copy(
                src_ref=to_l, dst_ref=dst.at[pl.ds(base + CAP_BLOCKS, CAP_BLOCKS)],
                send_sem=d_send.at[first, c], recv_sem=d_recv.at[first, c],
                device_id={"dp": left}, device_id_type=MESH,
            ),
            pltpu.make_async_remote_copy(
                src_ref=to_r, dst_ref=dst.at[pl.ds(base, CAP_BLOCKS)],
                send_sem=d_send.at[first + 1, c], recv_sem=d_recv.at[first + 1, c],
                device_id={"dp": right}, device_id_type=MESH,
            ),
        ]

    out_moves = [exchange(p[2], p[3], p[1], SRC_BLOCKS, 0, c) for c, p in enumerate(parts)]
    cot_moves = [exchange(p[7], p[8], p[6], OWN_BLOCKS, 2, c) for c, p in enumerate(parts)]

    left_send = [slot_source(to_left, left_begins, starts, b) for b in range(CAP_BLOCKS)]
    right_send = [slot_source(to_right, right_begins, starts, b) for b in range(CAP_BLOCKS)]
    for c, part in enumerate(parts):
        sout, lsend, rsend = part[0], part[2], part[3]
        forward(c)
        for block in range(CAP_BLOCKS):
            gather(rsend, block, sout, right_send[block])
        out_moves[c][1].start()
        for block in range(CAP_BLOCKS):
            gather(lsend, block, sout, left_send[block])
        if c == 0:
            pl.semaphore_wait(ready, 1)
        out_moves[c][0].start()

    pack_from = []
    for block in range(OWN_BLOCKS):
        shift = jnp.int32(0)
        for j in range(ENTRIES):
            for mine, base, offset, count in (
                (owners[j] == me_d, starts[j], offsets[j], counts[j]),
                (from_left[j], SRC_BLOCKS + fl_begins[j], l_offsets[j], l_counts[j]),
                (from_right[j], SRC_BLOCKS + CAP_BLOCKS + fr_begins[j], r_offsets[j], r_counts[j]),
            ):
                inside = mine & (offset <= block) & (block < offset + count)
                shift = jnp.where(inside, base - offset, shift)
        pack_from.append(block + shift)
    left_back = [slot_source(from_left, fl_begins, l_offsets, b) for b in range(CAP_BLOCKS)]
    right_back = [slot_source(from_right, fr_begins, r_offsets, b) for b in range(CAP_BLOCKS)]

    for c, part in enumerate(parts):
        cat, pack, cown, ccat, lret, rret = part[1], part[4], part[5], part[6], part[7], part[8]
        cot_local[c].wait()
        for copy in cot_copies[c]:
            copy.wait_recv()
        for block in range(CAP_BLOCKS):
            gather(rret, block, cown, right_back[block])
            gather(lret, block, cown, left_back[block])
        for copy in cot_moves[c]:
            copy.start()
        for copy in out_moves[c]:
            copy.wait_recv()
        for block in range(OWN_BLOCKS):
            gather(pack, block, cat, pack_from[block])
        for copy in out_copies[c]:
            copy.start()
        out_local[c].start()
        ccat[pl.ds(0, OWN_BLOCKS)] = cown[...]

    cot_from = []
    for block in range(SRC_BLOCKS):
        shift = jnp.int32(0)
        for j in range(ENTRIES):
            base = jnp.where(
                owners[j] == me_d,
                offsets[j],
                jnp.where(to_left[j], OWN_BLOCKS + left_begins[j], OWN_BLOCKS + CAP_BLOCKS + right_begins[j]),
            )
            shift = jnp.where(block >= starts[j], base - starts[j], shift)
        cot_from.append(block + shift)
    for c, part in enumerate(parts):
        ccat, csrc = part[6], part[9]
        for copy in cot_moves[c]:
            copy.wait_recv()
        for block in range(SRC_BLOCKS):
            gather(csrc, block, ccat, cot_from[block])
        backward(c)

    for c in range(len(CHUNKS)):
        for copy in cot_copies[c] + out_moves[c] + cot_moves[c] + out_copies[c]:
            copy.wait_send()
        for copy in out_copies[c]:
            copy.wait_recv()
        out_local[c].wait()


def store_kernel(a, b, c, d, a_out, b_out, c_out, d_out, sem):
    copies = [
        pltpu.make_async_copy(src, dst, sem.at[i])
        for i, (src, dst) in enumerate(((a, a_out), (b, b_out), (c, c_out), (d, d_out)))
    ]
    for copy in copies:
        copy.start()
    for copy in copies:
        copy.wait()


def per_device(queries, keys_in, values, q_gain, k_gain, cotangent, patch_counts, image_owner, pack_offset):
    n_dp, n_t = lax.axis_size("dp"), lax.axis_size("tensor")
    width = queries.shape[1]
    heads = width // HD
    grad_shape = queries.shape
    attn_shape = (cotangent.shape[0] // BLOCK, BLOCK, cotangent.shape[1])
    dma = pltpu.SemaphoreType.DMA
    n_c = len(CHUNKS)
    vmem = pltpu.VMEM

    def blocks(count, run):
        return vmem((count, BLOCK, run * HD), BF16)

    scratch = [
        vmem((SRC_ROWS, width), BF16), vmem((SRC_ROWS, width), BF16), vmem((SRC_ROWS, width), BF16),
        vmem((1, HD), F32), vmem((1, HD), F32),
        pltpu.SMEM((ENTRIES, n_dp), jnp.int32),
        pltpu.SMEM((ENTRIES, n_dp), jnp.int32),
        pltpu.SMEM((ENTRIES, n_dp), jnp.int32),
        vmem((heads, SRC_ROWS, HD), BF16), vmem((heads, SRC_ROWS, HD), BF16),
        vmem((heads, SRC_ROWS, HD), F32), vmem((heads, SRC_ROWS, HD), F32),
        vmem((heads, SRC_ROWS, HD), F32), vmem((heads, SRC_ROWS, HD), F32),
        vmem((heads, SRC_ROWS, SRC_ROWS), F32),
        vmem((SRC_ROWS, SRC_ROWS), F32),
        dma((5,)), dma((3,)), dma((2, n_c)),
        dma((n_c, n_t - 1)), dma((n_c, n_t - 1)), dma((n_c, n_t - 1)), dma((n_c, n_t - 1)),
        dma((4, n_c)), dma((4, n_c)), pltpu.SemaphoreType.REGULAR,
    ]
    for run in CHUNKS:
        scratch += [
            blocks(SRC_BLOCKS, run), blocks(SRC_BLOCKS + 2 * CAP_BLOCKS, run),
            blocks(CAP_BLOCKS, run), blocks(CAP_BLOCKS, run), blocks(OWN_BLOCKS, run),
            blocks(OWN_BLOCKS, run), blocks(OWN_BLOCKS + 2 * CAP_BLOCKS, run),
            blocks(CAP_BLOCKS, run), blocks(CAP_BLOCKS, run), blocks(SRC_BLOCKS, run),
        ]
    any_spec = pl.BlockSpec(memory_space=pl.ANY)
    vmem_spec = pl.BlockSpec(memory_space=pltpu.VMEM)
    flops = 12 * heads * SRC_ROWS * SRC_ROWS * HD
    operands = (
        queries, keys_in, values, cotangent.reshape(attn_shape), q_gain.reshape(1, HD), k_gain.reshape(1, HD),
        patch_counts.T, image_owner.T, pack_offset.T,
    )
    held = pl.pallas_call(
        functools.partial(kernel, n_dp, n_t, heads),
        out_shape=[vmem(attn_shape, BF16)] + [vmem(grad_shape, BF16)] * 3,
        in_specs=[any_spec] * 9,
        out_specs=[vmem_spec] * 4,
        scratch_shapes=scratch,
        compiler_params=pltpu.CompilerParams(
            collective_id=0, has_side_effects=True, vmem_limit_bytes=40 * 2**20
        ),
        cost_estimate=pl.CostEstimate(flops=flops, bytes_accessed=5 * 2**20, transcendentals=0),
    )(*[pltpu.with_memory_space_constraint(x, pltpu.HBM) for x in operands])
    held = [pltpu.with_memory_space_constraint(x, pltpu.VMEM) for x in held]
    attn_out, grad_q, grad_k, grad_v = pl.pallas_call(
        store_kernel,
        out_shape=[jax.ShapeDtypeStruct(x.shape, BF16) for x in held],
        in_specs=[vmem_spec] * 4,
        out_specs=[any_spec] * 4,
        scratch_shapes=[dma((4,))],
        compiler_params=pltpu.CompilerParams(vmem_limit_bytes=16 * 2**20),
        cost_estimate=pl.CostEstimate(flops=0, bytes_accessed=5 * 2**20, transcendentals=0),
    )(*held)
    return attn_out.reshape(cotangent.shape), grad_q, grad_k, grad_v


def solution(mesh):
    in_specs = (
        P("dp", "tensor"),
        P("dp", "tensor"),
        P("dp", "tensor"),
        P(),
        P(),
        P(("dp", "tensor"), None),
        P(),
        P(),
        P(),
    )
    out_specs = (P(("dp", "tensor"), None), P("dp", "tensor"), P("dp", "tensor"), P("dp", "tensor"))
    return jax.shard_map(
        per_device, mesh=mesh, in_specs=in_specs, out_specs=out_specs, check_vma=False
    )
```

```python
import functools

import jax
import jax.numpy as jnp
from jax import lax
from jax.experimental import pallas as pl
from jax.experimental.pallas import tpu as pltpu
from jax.sharding import PartitionSpec as P

MESH = pl.DeviceIdType.MESH
HD = 128
OWN_ROWS = 256
CAP = 96
SRC_ROWS = 448
ENTRIES = 6
BLOCK = 16
OWN_BLOCKS = OWN_ROWS // BLOCK
CAP_BLOCKS = CAP // BLOCK
SRC_BLOCKS = SRC_ROWS // BLOCK
CHUNKS = (2, 2, 2)
LOG2E = 1.4426950408889634
EPS = 1e-06
BF16 = jnp.bfloat16
F32 = jnp.float32


def begins_of(counts, owners, wanted):
    begins, total = [], jnp.int32(0)
    chosen = [owner == wanted for owner in owners]
    for count, mine in zip(counts, chosen):
        begins.append(total)
        total = total + jnp.where(mine, count, 0)
    return chosen, begins


def slot_source(chosen, begins, targets, block):
    shift = jnp.int32(0)
    for mine, begin, target in zip(chosen, begins, targets):
        shift = jnp.where(mine & (block >= begin), target - begin, shift)
    return block + shift


def lane_mean(x):
    return jnp.sum(x, axis=-1, keepdims=True) * (1.0 / HD)


def normalize(x):
    centred = x - lane_mean(x)
    inverse = lax.rsqrt(lane_mean(centred * centred) + EPS)
    return centred * inverse, inverse


def norm_back(grad, normed, inverse, gain):
    scaled = grad * gain
    first = lane_mean(scaled)
    second = lane_mean(scaled * normed)
    return inverse * (scaled - first - normed * second)


def dot(a, b, dims):
    return lax.dot_general(a, b, (dims, ((), ())), preferred_element_type=F32)


def kernel(n_dp, n_t, heads, *refs):
    (q_hbm, k_hbm, v_hbm, cot_hbm, qg_hbm, kg_hbm, cnt_hbm, own_hbm, off_hbm) = refs[:9]
    attn, gq_out, gk_out, gv_out = refs[9:13]
    (q_in, k_in, v_in, qg, kg, cnt, own, off, qn, kn, qh, kh, qi, ki, w_s, bias) = refs[13:29]
    in_sem, tab_sem, local_sem, a_send, a_recv, b_send, b_recv, d_send, d_recv, ready = refs[29:39]
    parts = [refs[39 + 10 * c: 49 + 10 * c] for c in range(len(CHUNKS))]
    firsts = [sum(CHUNKS[:c]) for c in range(len(CHUNKS))]

    me_d = lax.axis_index("dp")
    me_t = lax.axis_index("tensor")
    left = lax.rem(me_d + n_dp - 1, n_dp)
    right = lax.rem(me_d + 1, n_dp)
    width = heads * HD
    blocks_t = OWN_BLOCKS // n_t
    steps = sorted(range(1, n_t), key=lambda s: (-min(s, n_t - s), s))
    peers = [lax.rem(me_t + s, n_t) for s in steps]

    tables = [
        pltpu.make_async_copy(src, dst, tab_sem.at[i])
        for i, (src, dst) in enumerate([(cnt_hbm, cnt), (own_hbm, own), (off_hbm, off)])
    ]
    loads = [
        pltpu.make_async_copy(src, dst, in_sem.at[i])
        for i, (src, dst) in enumerate(
            [(q_hbm, q_in), (k_hbm, k_in), (v_hbm, v_in), (qg_hbm, qg), (kg_hbm, kg)]
        )
    ]
    barrier = pltpu.get_barrier_semaphore()
    for peer in peers:
        pl.semaphore_signal(barrier, inc=1, device_id={"tensor": peer}, device_id_type=MESH)
    pl.semaphore_signal(barrier, inc=1, device_id={"dp": left}, device_id_type=MESH)
    for copy in tables + loads:
        copy.start()
    pl.semaphore_wait(barrier, n_t)
    pl.semaphore_signal(ready, inc=1, device_id={"dp": right}, device_id_type=MESH)

    def cols(index, c):
        return pl.ds(pl.multiple_of(index * width + firsts[c] * HD, HD), CHUNKS[c] * HD)

    def token_blocks(index):
        return pl.ds(index * blocks_t, blocks_t)

    cot_copies, out_copies, cot_local, out_local = [], [], [], []
    for c, part in enumerate(parts):
        pack, cown = part[4], part[5]
        cot_copies.append([
            pltpu.make_async_remote_copy(
                src_ref=cot_hbm.at[:, :, cols(peer, c)], dst_ref=cown.at[token_blocks(me_t)],
                send_sem=a_send.at[c, i], recv_sem=a_recv.at[c, i],
                device_id={"tensor": peer}, device_id_type=MESH,
            )
            for i, peer in enumerate(peers)
        ])
        cot_local.append(pltpu.make_async_copy(
            cot_hbm.at[:, :, cols(me_t, c)], cown.at[token_blocks(me_t)], local_sem.at[0, c]
        ))
        out_copies.append([
            pltpu.make_async_remote_copy(
                src_ref=pack.at[token_blocks(peer)], dst_ref=attn.at[:, :, cols(me_t, c)],
                send_sem=b_send.at[c, i], recv_sem=b_recv.at[c, i],
                device_id={"tensor": peer}, device_id_type=MESH,
            )
            for i, peer in enumerate(peers)
        ])
        out_local.append(pltpu.make_async_copy(
            pack.at[token_blocks(me_t)], attn.at[:, :, cols(me_t, c)], local_sem.at[1, c]
        ))
    def send_cot():
        for c in range(len(CHUNKS)):
            for copy in cot_copies[c]:
                copy.start()

    odd = lax.rem(me_d, 2) == 1
    pl.when(odd)(send_cot)
    for c in range(len(CHUNKS)):
        cot_local[c].start()

    for copy in tables:
        copy.wait()

    def entries(source):
        counts = [cnt[j, source] >> 4 for j in range(ENTRIES)]
        owners = [own[j, source] for j in range(ENTRIES)]
        offsets = [off[j, source] >> 4 for j in range(ENTRIES)]
        return counts, owners, offsets

    counts, owners, offsets = entries(me_d)
    l_counts, l_owners, l_offsets = entries(left)
    r_counts, r_owners, r_offsets = entries(right)
    starts, ends, total = [], [], jnp.int32(0)
    for count in counts:
        starts.append(total)
        total = total + count
        ends.append(total)
    to_left, left_begins = begins_of(counts, owners, left)
    to_right, right_begins = begins_of(counts, owners, right)
    from_left, fl_begins = begins_of(l_counts, l_owners, me_d)
    from_right, fr_begins = begins_of(r_counts, r_owners, me_d)

    def segments(axis):
        row = lax.broadcasted_iota(jnp.int32, (SRC_ROWS, 1) if axis == 0 else (1, SRC_ROWS), axis)
        segment = jnp.zeros(row.shape, jnp.int32)
        for end in ends:
            segment = segment + (row >= end * BLOCK).astype(jnp.int32)
        return segment

    bias[...] = jnp.where(segments(0) == segments(1), 0.0, -1e30).astype(F32)
    in_use = lax.broadcasted_iota(jnp.int32, (SRC_ROWS, 1), 0) < total * BLOCK

    for copy in loads:
        copy.wait()

    scale = HD ** -0.5

    def forward(c):
        sout, cat = parts[c][0], parts[c][1]
        for h in range(firsts[c], firsts[c] + CHUNKS[c]):
            lanes = pl.ds(h * HD, HD)
            query_hat, query_inv = normalize(q_in[:, lanes].astype(F32))
            key_hat, key_inv = normalize(k_in[:, lanes].astype(F32))
            qh[h] = query_hat
            kh[h] = key_hat
            qi[h] = jnp.broadcast_to(query_inv, (SRC_ROWS, HD))
            ki[h] = jnp.broadcast_to(key_inv, (SRC_ROWS, HD))
            query_norm = (query_hat * qg[...]).astype(BF16)
            key_norm = (key_hat * kg[...]).astype(BF16)
            qn[h] = query_norm
            kn[h] = key_norm
            scores = dot(key_norm, query_norm, ((1,), (1,))) + bias[...]
            powers = jnp.exp2((scores - jnp.max(scores, axis=0, keepdims=True)) * (scale * LOG2E))
            weights = powers * (1.0 / jnp.sum(powers, axis=0, keepdims=True))
            w_s[h] = weights
            out = dot(weights.astype(BF16), v_in[:, lanes], ((0,), (0,))).astype(BF16)
            out = out.reshape(SRC_BLOCKS, BLOCK, HD)
            local = pl.ds((h - firsts[c]) * HD, HD)
            sout[:, :, local] = out
            cat[pl.ds(0, SRC_BLOCKS), :, local] = out

    def backward(c):
        csrc = parts[c][9]
        for h in range(firsts[c], firsts[c] + CHUNKS[c]):
            lanes = pl.ds(h * HD, HD)
            cot = csrc[:, :, pl.ds((h - firsts[c]) * HD, HD)].reshape(SRC_ROWS, HD)
            weights = w_s[h]
            grad_w = dot(v_in[:, lanes], cot, ((1,), (1,)))
            inner = jnp.sum(weights * grad_w, axis=0, keepdims=True)
            grad_s = (weights * (grad_w - inner) * scale).astype(BF16)
            grad_v = dot(weights.astype(BF16), cot, ((1,), (0,)))
            grad_k = dot(grad_s, qn[h], ((1,), (0,)))
            grad_q = dot(grad_s, kn[h], ((0,), (0,)))
            grad_q = norm_back(grad_q, qh[h], qi[h], qg[...])
            grad_k = norm_back(grad_k, kh[h], ki[h], kg[...])
            gq_out[:, lanes] = jnp.where(in_use, grad_q, 0.0).astype(BF16)
            gk_out[:, lanes] = jnp.where(in_use, grad_k, 0.0).astype(BF16)
            gv_out[:, lanes] = jnp.where(in_use, grad_v, 0.0).astype(BF16)

    def gather(dst, block, src, index):
        dst[block] = src[jnp.clip(index, 0, src.shape[0] - 1)]

    def exchange(to_l, to_r, dst, base, first, c):
        return [
            pltpu.make_async_remote_copy(
                src_ref=to_l, dst_ref=dst.at[pl.ds(base + CAP_BLOCKS, CAP_BLOCKS)],
                send_sem=d_send.at[first, c], recv_sem=d_recv.at[first, c],
                device_id={"dp": left}, device_id_type=MESH,
            ),
            pltpu.make_async_remote_copy(
                src_ref=to_r, dst_ref=dst.at[pl.ds(base, CAP_BLOCKS)],
                send_sem=d_send.at[first + 1, c], recv_sem=d_recv.at[first + 1, c],
                device_id={"dp": right}, device_id_type=MESH,
            ),
        ]

    out_moves = [exchange(p[2], p[3], p[1], SRC_BLOCKS, 0, c) for c, p in enumerate(parts)]
    cot_moves = [exchange(p[7], p[8], p[6], OWN_BLOCKS, 2, c) for c, p in enumerate(parts)]

    left_send = [slot_source(to_left, left_begins, starts, b) for b in range(CAP_BLOCKS)]
    right_send = [slot_source(to_right, right_begins, starts, b) for b in range(CAP_BLOCKS)]
    for c, part in enumerate(parts):
        sout, lsend, rsend = part[0], part[2], part[3]
        forward(c)
        if c == 1:
            pl.when(jnp.logical_not(odd))(send_cot)
        for block in range(CAP_BLOCKS):
            gather(rsend, block, sout, right_send[block])
        out_moves[c][1].start()
        for block in range(CAP_BLOCKS):
            gather(lsend, block, sout, left_send[block])
        if c == 1:
            pl.semaphore_wait(ready, 1)
            for move in out_moves[:c]:
                move[0].start()
        if c >= 1:
            out_moves[c][0].start()

    pack_from = []
    for block in range(OWN_BLOCKS):
        shift = jnp.int32(0)
        for j in range(ENTRIES):
            for mine, base, offset, count in (
                (owners[j] == me_d, starts[j], offsets[j], counts[j]),
                (from_left[j], SRC_BLOCKS + fl_begins[j], l_offsets[j], l_counts[j]),
                (from_right[j], SRC_BLOCKS + CAP_BLOCKS + fr_begins[j], r_offsets[j], r_counts[j]),
            ):
                inside = mine & (offset <= block) & (block < offset + count)
                shift = jnp.where(inside, base - offset, shift)
        pack_from.append(block + shift)
    left_back = [slot_source(from_left, fl_begins, l_offsets, b) for b in range(CAP_BLOCKS)]
    right_back = [slot_source(from_right, fr_begins, r_offsets, b) for b in range(CAP_BLOCKS)]

    for c, part in enumerate(parts):
        cat, pack, cown, ccat, lret, rret = part[1], part[4], part[5], part[6], part[7], part[8]
        cot_local[c].wait()
        for copy in cot_copies[c]:
            copy.wait_recv()
        for block in range(CAP_BLOCKS):
            gather(rret, block, cown, right_back[block])
            gather(lret, block, cown, left_back[block])
        for copy in cot_moves[c]:
            copy.start()
        for copy in out_moves[c]:
            copy.wait_recv()
        for block in range(OWN_BLOCKS):
            gather(pack, block, cat, pack_from[block])
        for copy in out_copies[c]:
            copy.start()
        out_local[c].start()
        ccat[pl.ds(0, OWN_BLOCKS)] = cown[...]

    cot_from = []
    for block in range(SRC_BLOCKS):
        shift = jnp.int32(0)
        for j in range(ENTRIES):
            base = jnp.where(
                owners[j] == me_d,
                offsets[j],
                jnp.where(to_left[j], OWN_BLOCKS + left_begins[j], OWN_BLOCKS + CAP_BLOCKS + right_begins[j]),
            )
            shift = jnp.where(block >= starts[j], base - starts[j], shift)
        cot_from.append(block + shift)
    for c, part in enumerate(parts):
        ccat, csrc = part[6], part[9]
        for copy in cot_moves[c]:
            copy.wait_recv()
        for block in range(SRC_BLOCKS):
            gather(csrc, block, ccat, cot_from[block])
        backward(c)

    for c in range(len(CHUNKS)):
        for copy in cot_copies[c] + out_moves[c] + cot_moves[c] + out_copies[c]:
            copy.wait_send()
        for copy in out_copies[c]:
            copy.wait_recv()
        out_local[c].wait()


def store_kernel(a, b, c, d, a_out, b_out, c_out, d_out, sem):
    copies = [
        pltpu.make_async_copy(src, dst, sem.at[i])
        for i, (src, dst) in enumerate(((a, a_out), (b, b_out), (c, c_out), (d, d_out)))
    ]
    for copy in copies:
        copy.start()
    for copy in copies:
        copy.wait()


def per_device(queries, keys_in, values, q_gain, k_gain, cotangent, patch_counts, image_owner, pack_offset):
    n_dp, n_t = lax.axis_size("dp"), lax.axis_size("tensor")
    width = queries.shape[1]
    heads = width // HD
    grad_shape = queries.shape
    attn_shape = (cotangent.shape[0] // BLOCK, BLOCK, cotangent.shape[1])
    dma = pltpu.SemaphoreType.DMA
    n_c = len(CHUNKS)
    vmem = pltpu.VMEM

    def blocks(count, run):
        return vmem((count, BLOCK, run * HD), BF16)

    scratch = [
        vmem((SRC_ROWS, width), BF16), vmem((SRC_ROWS, width), BF16), vmem((SRC_ROWS, width), BF16),
        vmem((1, HD), F32), vmem((1, HD), F32),
        pltpu.SMEM((ENTRIES, n_dp), jnp.int32),
        pltpu.SMEM((ENTRIES, n_dp), jnp.int32),
        pltpu.SMEM((ENTRIES, n_dp), jnp.int32),
        vmem((heads, SRC_ROWS, HD), BF16), vmem((heads, SRC_ROWS, HD), BF16),
        vmem((heads, SRC_ROWS, HD), F32), vmem((heads, SRC_ROWS, HD), F32),
        vmem((heads, SRC_ROWS, HD), F32), vmem((heads, SRC_ROWS, HD), F32),
        vmem((heads, SRC_ROWS, SRC_ROWS), F32),
        vmem((SRC_ROWS, SRC_ROWS), F32),
        dma((5,)), dma((3,)), dma((2, n_c)),
        dma((n_c, n_t - 1)), dma((n_c, n_t - 1)), dma((n_c, n_t - 1)), dma((n_c, n_t - 1)),
        dma((4, n_c)), dma((4, n_c)), pltpu.SemaphoreType.REGULAR,
    ]
    for run in CHUNKS:
        scratch += [
            blocks(SRC_BLOCKS, run), blocks(SRC_BLOCKS + 2 * CAP_BLOCKS, run),
            blocks(CAP_BLOCKS, run), blocks(CAP_BLOCKS, run), blocks(OWN_BLOCKS, run),
            blocks(OWN_BLOCKS, run), blocks(OWN_BLOCKS + 2 * CAP_BLOCKS, run),
            blocks(CAP_BLOCKS, run), blocks(CAP_BLOCKS, run), blocks(SRC_BLOCKS, run),
        ]
    any_spec = pl.BlockSpec(memory_space=pl.ANY)
    vmem_spec = pl.BlockSpec(memory_space=pltpu.VMEM)
    flops = 12 * heads * SRC_ROWS * SRC_ROWS * HD
    operands = (
        queries, keys_in, values, cotangent.reshape(attn_shape), q_gain.reshape(1, HD), k_gain.reshape(1, HD),
        patch_counts.T, image_owner.T, pack_offset.T,
    )
    held = pl.pallas_call(
        functools.partial(kernel, n_dp, n_t, heads),
        out_shape=[vmem(attn_shape, BF16)] + [vmem(grad_shape, BF16)] * 3,
        in_specs=[any_spec] * 9,
        out_specs=[vmem_spec] * 4,
        scratch_shapes=scratch,
        compiler_params=pltpu.CompilerParams(
            collective_id=0, has_side_effects=True, vmem_limit_bytes=40 * 2**20
        ),
        cost_estimate=pl.CostEstimate(flops=flops, bytes_accessed=5 * 2**20, transcendentals=0),
    )(*[pltpu.with_memory_space_constraint(x, pltpu.HBM) for x in operands])
    held = [pltpu.with_memory_space_constraint(x, pltpu.VMEM) for x in held]
    attn_out, grad_q, grad_k, grad_v = pl.pallas_call(
        store_kernel,
        out_shape=[jax.ShapeDtypeStruct(x.shape, BF16) for x in held],
        in_specs=[vmem_spec] * 4,
        out_specs=[any_spec] * 4,
        scratch_shapes=[dma((4,))],
        compiler_params=pltpu.CompilerParams(vmem_limit_bytes=16 * 2**20),
        cost_estimate=pl.CostEstimate(flops=0, bytes_accessed=5 * 2**20, transcendentals=0),
    )(*held)
    return attn_out.reshape(cotangent.shape), grad_q, grad_k, grad_v


def solution(mesh):
    in_specs = (
        P("dp", "tensor"),
        P("dp", "tensor"),
        P("dp", "tensor"),
        P(),
        P(),
        P(("dp", "tensor"), None),
        P(),
        P(),
        P(),
    )
    out_specs = (P(("dp", "tensor"), None), P("dp", "tensor"), P("dp", "tensor"), P("dp", "tensor"))
    return jax.shard_map(
        per_device, mesh=mesh, in_specs=in_specs, out_specs=out_specs, check_vma=False
    )
```

```python
import functools

import jax
import jax.numpy as jnp
from jax import lax
from jax.experimental import pallas as pl
from jax.experimental.pallas import tpu as pltpu
from jax.sharding import PartitionSpec as P

MESH = pl.DeviceIdType.MESH
HD = 128
OWN_ROWS = 256
CAP = 96
SRC_ROWS = 448
ENTRIES = 6
BLOCK = 16
OWN_BLOCKS = OWN_ROWS // BLOCK
CAP_BLOCKS = CAP // BLOCK
SRC_BLOCKS = SRC_ROWS // BLOCK
CHUNKS = (2, 2, 2)
LOG2E = 1.4426950408889634
EPS = 1e-06
BF16 = jnp.bfloat16
F32 = jnp.float32


def begins_of(counts, owners, wanted):
    begins, total = [], jnp.int32(0)
    chosen = [owner == wanted for owner in owners]
    for count, mine in zip(counts, chosen):
        begins.append(total)
        total = total + jnp.where(mine, count, 0)
    return chosen, begins


def slot_source(chosen, begins, targets, block):
    shift = jnp.int32(0)
    for mine, begin, target in zip(chosen, begins, targets):
        shift = jnp.where(mine & (block >= begin), target - begin, shift)
    return block + shift


def lane_mean(x):
    return jnp.sum(x, axis=-1, keepdims=True) * (1.0 / HD)


def normalize(x):
    centred = x - lane_mean(x)
    inverse = lax.rsqrt(lane_mean(centred * centred) + EPS)
    return centred * inverse, inverse


def norm_back(grad, normed, inverse, gain):
    scaled = grad * gain
    first = lane_mean(scaled)
    second = lane_mean(scaled * normed)
    return inverse * (scaled - first - normed * second)


def dot(a, b, dims):
    return lax.dot_general(a, b, (dims, ((), ())), preferred_element_type=F32)


def kernel(n_dp, n_t, heads, *refs):
    (q_hbm, k_hbm, v_hbm, cot_hbm, qg_hbm, kg_hbm, cnt_hbm, own_hbm, off_hbm) = refs[:9]
    attn, gq_out, gk_out, gv_out = refs[9:13]
    (q_in, k_in, v_in, qg, kg, cnt, own, off, qn, kn, qh, kh, qi, ki, w_s, bias) = refs[13:29]
    in_sem, tab_sem, local_sem, a_send, a_recv, b_send, b_recv, d_send, d_recv, ready = refs[29:39]
    parts = [refs[39 + 10 * c: 49 + 10 * c] for c in range(len(CHUNKS))]
    firsts = [sum(CHUNKS[:c]) for c in range(len(CHUNKS))]

    me_d = lax.axis_index("dp")
    me_t = lax.axis_index("tensor")
    left = lax.rem(me_d + n_dp - 1, n_dp)
    right = lax.rem(me_d + 1, n_dp)
    width = heads * HD
    blocks_t = OWN_BLOCKS // n_t
    steps = sorted(range(1, n_t), key=lambda s: (-min(s, n_t - s), s))
    peers = [lax.rem(me_t + s, n_t) for s in steps]

    tables = [
        pltpu.make_async_copy(src, dst, tab_sem.at[i])
        for i, (src, dst) in enumerate([(cnt_hbm, cnt), (own_hbm, own), (off_hbm, off)])
    ]
    loads = [
        pltpu.make_async_copy(src, dst, in_sem.at[i])
        for i, (src, dst) in enumerate(
            [(q_hbm, q_in), (k_hbm, k_in), (v_hbm, v_in), (qg_hbm, qg), (kg_hbm, kg)]
        )
    ]
    barrier = pltpu.get_barrier_semaphore()
    for peer in peers:
        pl.semaphore_signal(barrier, inc=1, device_id={"tensor": peer}, device_id_type=MESH)
    pl.semaphore_signal(barrier, inc=1, device_id={"dp": left}, device_id_type=MESH)
    for copy in tables + loads:
        copy.start()

    def cols(index, c):
        return pl.ds(pl.multiple_of(index * width + firsts[c] * HD, HD), CHUNKS[c] * HD)

    def token_blocks(index):
        return pl.ds(index * blocks_t, blocks_t)

    cot_copies, out_copies, cot_local, out_local = [], [], [], []
    for c, part in enumerate(parts):
        pack, cown = part[4], part[5]
        cot_copies.append([
            pltpu.make_async_remote_copy(
                src_ref=cot_hbm.at[:, :, cols(peer, c)], dst_ref=cown.at[token_blocks(me_t)],
                send_sem=a_send.at[c, i], recv_sem=a_recv.at[c, i],
                device_id={"tensor": peer}, device_id_type=MESH,
            )
            for i, peer in enumerate(peers)
        ])
        cot_local.append(pltpu.make_async_copy(
            cot_hbm.at[:, :, cols(me_t, c)], cown.at[token_blocks(me_t)], local_sem.at[0, c]
        ))
        out_copies.append([
            pltpu.make_async_remote_copy(
                src_ref=pack.at[token_blocks(peer)], dst_ref=attn.at[:, :, cols(me_t, c)],
                send_sem=b_send.at[c, i], recv_sem=b_recv.at[c, i],
                device_id={"tensor": peer}, device_id_type=MESH,
            )
            for i, peer in enumerate(peers)
        ])
        out_local.append(pltpu.make_async_copy(
            pack.at[token_blocks(me_t)], attn.at[:, :, cols(me_t, c)], local_sem.at[1, c]
        ))
    for copy in tables:
        copy.wait()

    def entries(source):
        counts = [cnt[j, source] >> 4 for j in range(ENTRIES)]
        owners = [own[j, source] for j in range(ENTRIES)]
        offsets = [off[j, source] >> 4 for j in range(ENTRIES)]
        return counts, owners, offsets

    counts, owners, offsets = entries(me_d)
    l_counts, l_owners, l_offsets = entries(left)
    r_counts, r_owners, r_offsets = entries(right)
    starts, ends, total = [], [], jnp.int32(0)
    for count in counts:
        starts.append(total)
        total = total + count
        ends.append(total)
    to_left, left_begins = begins_of(counts, owners, left)
    to_right, right_begins = begins_of(counts, owners, right)
    from_left, fl_begins = begins_of(l_counts, l_owners, me_d)
    from_right, fr_begins = begins_of(r_counts, r_owners, me_d)

    def segments(axis):
        row = lax.broadcasted_iota(jnp.int32, (SRC_ROWS, 1) if axis == 0 else (1, SRC_ROWS), axis)
        segment = jnp.zeros(row.shape, jnp.int32)
        for end in ends:
            segment = segment + (row >= end * BLOCK).astype(jnp.int32)
        return segment

    bias[...] = jnp.where(segments(0) == segments(1), 0.0, -1e30).astype(F32)
    in_use = lax.broadcasted_iota(jnp.int32, (SRC_ROWS, 1), 0) < total * BLOCK

    pl.semaphore_wait(barrier, n_t)
    pl.semaphore_signal(ready, inc=1, device_id={"dp": right}, device_id_type=MESH)

    def send_cot():
        for c in range(len(CHUNKS)):
            for copy in cot_copies[c]:
                copy.start()

    odd = lax.rem(me_d, 2) == 1
    pl.when(odd)(send_cot)
    for c in range(len(CHUNKS)):
        cot_local[c].start()

    for copy in loads:
        copy.wait()

    scale = HD ** -0.5

    def forward(c):
        sout, cat = parts[c][0], parts[c][1]
        for h in range(firsts[c], firsts[c] + CHUNKS[c]):
            lanes = pl.ds(h * HD, HD)
            query_hat, query_inv = normalize(q_in[:, lanes].astype(F32))
            key_hat, key_inv = normalize(k_in[:, lanes].astype(F32))
            qh[h] = query_hat
            kh[h] = key_hat
            qi[h] = jnp.broadcast_to(query_inv, (SRC_ROWS, HD))
            ki[h] = jnp.broadcast_to(key_inv, (SRC_ROWS, HD))
            query_norm = (query_hat * qg[...]).astype(BF16)
            key_norm = (key_hat * kg[...]).astype(BF16)
            qn[h] = query_norm
            kn[h] = key_norm
            scores = dot(key_norm, query_norm, ((1,), (1,))) + bias[...]
            powers = jnp.exp2((scores - jnp.max(scores, axis=0, keepdims=True)) * (scale * LOG2E))
            weights = powers * (1.0 / jnp.sum(powers, axis=0, keepdims=True))
            w_s[h] = weights
            out = dot(weights.astype(BF16), v_in[:, lanes], ((0,), (0,))).astype(BF16)
            out = out.reshape(SRC_BLOCKS, BLOCK, HD)
            local = pl.ds((h - firsts[c]) * HD, HD)
            sout[:, :, local] = out
            cat[pl.ds(0, SRC_BLOCKS), :, local] = out

    def backward(c):
        csrc = parts[c][9]
        for h in range(firsts[c], firsts[c] + CHUNKS[c]):
            lanes = pl.ds(h * HD, HD)
            cot = csrc[:, :, pl.ds((h - firsts[c]) * HD, HD)].reshape(SRC_ROWS, HD)
            weights = w_s[h]
            grad_w = dot(v_in[:, lanes], cot, ((1,), (1,)))
            inner = jnp.sum(weights * grad_w, axis=0, keepdims=True)
            grad_s = (weights * (grad_w - inner) * scale).astype(BF16)
            grad_v = dot(weights.astype(BF16), cot, ((1,), (0,)))
            grad_k = dot(grad_s, qn[h], ((1,), (0,)))
            grad_q = dot(grad_s, kn[h], ((0,), (0,)))
            grad_q = norm_back(grad_q, qh[h], qi[h], qg[...])
            grad_k = norm_back(grad_k, kh[h], ki[h], kg[...])
            gq_out[:, lanes] = jnp.where(in_use, grad_q, 0.0).astype(BF16)
            gk_out[:, lanes] = jnp.where(in_use, grad_k, 0.0).astype(BF16)
            gv_out[:, lanes] = jnp.where(in_use, grad_v, 0.0).astype(BF16)

    def gather(dst, block, src, index):
        dst[block] = src[jnp.clip(index, 0, src.shape[0] - 1)]

    def exchange(to_l, to_r, dst, base, first, c):
        return [
            pltpu.make_async_remote_copy(
                src_ref=to_l, dst_ref=dst.at[pl.ds(base + CAP_BLOCKS, CAP_BLOCKS)],
                send_sem=d_send.at[first, c], recv_sem=d_recv.at[first, c],
                device_id={"dp": left}, device_id_type=MESH,
            ),
            pltpu.make_async_remote_copy(
                src_ref=to_r, dst_ref=dst.at[pl.ds(base, CAP_BLOCKS)],
                send_sem=d_send.at[first + 1, c], recv_sem=d_recv.at[first + 1, c],
                device_id={"dp": right}, device_id_type=MESH,
            ),
        ]

    out_moves = [exchange(p[2], p[3], p[1], SRC_BLOCKS, 0, c) for c, p in enumerate(parts)]
    cot_moves = [exchange(p[7], p[8], p[6], OWN_BLOCKS, 2, c) for c, p in enumerate(parts)]

    left_send = [slot_source(to_left, left_begins, starts, b) for b in range(CAP_BLOCKS)]
    right_send = [slot_source(to_right, right_begins, starts, b) for b in range(CAP_BLOCKS)]
    for c, part in enumerate(parts):
        sout, lsend, rsend = part[0], part[2], part[3]
        forward(c)
        if c == 1:
            pl.when(jnp.logical_not(odd))(send_cot)
        for block in range(CAP_BLOCKS):
            gather(rsend, block, sout, right_send[block])
        out_moves[c][1].start()
        for block in range(CAP_BLOCKS):
            gather(lsend, block, sout, left_send[block])
        if c == 1:
            pl.semaphore_wait(ready, 1)
            for move in out_moves[:c]:
                move[0].start()
        if c >= 1:
            out_moves[c][0].start()

    pack_from = []
    for block in range(OWN_BLOCKS):
        shift = jnp.int32(0)
        for j in range(ENTRIES):
            for mine, base, offset, count in (
                (owners[j] == me_d, starts[j], offsets[j], counts[j]),
                (from_left[j], SRC_BLOCKS + fl_begins[j], l_offsets[j], l_counts[j]),
                (from_right[j], SRC_BLOCKS + CAP_BLOCKS + fr_begins[j], r_offsets[j], r_counts[j]),
            ):
                inside = mine & (offset <= block) & (block < offset + count)
                shift = jnp.where(inside, base - offset, shift)
        pack_from.append(block + shift)
    left_back = [slot_source(from_left, fl_begins, l_offsets, b) for b in range(CAP_BLOCKS)]
    right_back = [slot_source(from_right, fr_begins, r_offsets, b) for b in range(CAP_BLOCKS)]

    for c, part in enumerate(parts):
        cat, pack, cown, ccat, lret, rret = part[1], part[4], part[5], part[6], part[7], part[8]
        cot_local[c].wait()
        for copy in cot_copies[c]:
            copy.wait_recv()
        for block in range(CAP_BLOCKS):
            gather(rret, block, cown, right_back[block])
            gather(lret, block, cown, left_back[block])
        for copy in cot_moves[c]:
            copy.start()
        for copy in out_moves[c]:
            copy.wait_recv()
        for block in range(OWN_BLOCKS):
            gather(pack, block, cat, pack_from[block])
        for copy in out_copies[c]:
            copy.start()
        out_local[c].start()
        ccat[pl.ds(0, OWN_BLOCKS)] = cown[...]

    cot_from = []
    for block in range(SRC_BLOCKS):
        shift = jnp.int32(0)
        for j in range(ENTRIES):
            base = jnp.where(
                owners[j] == me_d,
                offsets[j],
                jnp.where(to_left[j], OWN_BLOCKS + left_begins[j], OWN_BLOCKS + CAP_BLOCKS + right_begins[j]),
            )
            shift = jnp.where(block >= starts[j], base - starts[j], shift)
        cot_from.append(block + shift)
    for c, part in enumerate(parts):
        ccat, csrc = part[6], part[9]
        for copy in cot_moves[c]:
            copy.wait_recv()
        for block in range(SRC_BLOCKS):
            gather(csrc, block, ccat, cot_from[block])
        backward(c)

    for c in range(len(CHUNKS)):
        for copy in cot_copies[c] + out_moves[c] + cot_moves[c] + out_copies[c]:
            copy.wait_send()
        for copy in out_copies[c]:
            copy.wait_recv()
        out_local[c].wait()


def store_kernel(a, b, c, d, a_out, b_out, c_out, d_out, sem):
    copies = [
        pltpu.make_async_copy(src, dst, sem.at[i])
        for i, (src, dst) in enumerate(((a, a_out), (b, b_out), (c, c_out), (d, d_out)))
    ]
    for copy in copies:
        copy.start()
    for copy in copies:
        copy.wait()


def per_device(queries, keys_in, values, q_gain, k_gain, cotangent, patch_counts, image_owner, pack_offset):
    n_dp, n_t = lax.axis_size("dp"), lax.axis_size("tensor")
    width = queries.shape[1]
    heads = width // HD
    grad_shape = queries.shape
    attn_shape = (cotangent.shape[0] // BLOCK, BLOCK, cotangent.shape[1])
    dma = pltpu.SemaphoreType.DMA
    n_c = len(CHUNKS)
    vmem = pltpu.VMEM

    def blocks(count, run):
        return vmem((count, BLOCK, run * HD), BF16)

    scratch = [
        vmem((SRC_ROWS, width), BF16), vmem((SRC_ROWS, width), BF16), vmem((SRC_ROWS, width), BF16),
        vmem((1, HD), F32), vmem((1, HD), F32),
        pltpu.SMEM((ENTRIES, n_dp), jnp.int32),
        pltpu.SMEM((ENTRIES, n_dp), jnp.int32),
        pltpu.SMEM((ENTRIES, n_dp), jnp.int32),
        vmem((heads, SRC_ROWS, HD), BF16), vmem((heads, SRC_ROWS, HD), BF16),
        vmem((heads, SRC_ROWS, HD), F32), vmem((heads, SRC_ROWS, HD), F32),
        vmem((heads, SRC_ROWS, HD), F32), vmem((heads, SRC_ROWS, HD), F32),
        vmem((heads, SRC_ROWS, SRC_ROWS), F32),
        vmem((SRC_ROWS, SRC_ROWS), F32),
        dma((5,)), dma((3,)), dma((2, n_c)),
        dma((n_c, n_t - 1)), dma((n_c, n_t - 1)), dma((n_c, n_t - 1)), dma((n_c, n_t - 1)),
        dma((4, n_c)), dma((4, n_c)), pltpu.SemaphoreType.REGULAR,
    ]
    for run in CHUNKS:
        scratch += [
            blocks(SRC_BLOCKS, run), blocks(SRC_BLOCKS + 2 * CAP_BLOCKS, run),
            blocks(CAP_BLOCKS, run), blocks(CAP_BLOCKS, run), blocks(OWN_BLOCKS, run),
            blocks(OWN_BLOCKS, run), blocks(OWN_BLOCKS + 2 * CAP_BLOCKS, run),
            blocks(CAP_BLOCKS, run), blocks(CAP_BLOCKS, run), blocks(SRC_BLOCKS, run),
        ]
    any_spec = pl.BlockSpec(memory_space=pl.ANY)
    vmem_spec = pl.BlockSpec(memory_space=pltpu.VMEM)
    flops = 12 * heads * SRC_ROWS * SRC_ROWS * HD
    operands = (
        queries, keys_in, values, cotangent.reshape(attn_shape), q_gain.reshape(1, HD), k_gain.reshape(1, HD),
        patch_counts.T, image_owner.T, pack_offset.T,
    )
    held = pl.pallas_call(
        functools.partial(kernel, n_dp, n_t, heads),
        out_shape=[vmem(attn_shape, BF16)] + [vmem(grad_shape, BF16)] * 3,
        in_specs=[any_spec] * 9,
        out_specs=[vmem_spec] * 4,
        scratch_shapes=scratch,
        compiler_params=pltpu.CompilerParams(
            collective_id=0, has_side_effects=True, vmem_limit_bytes=40 * 2**20
        ),
        cost_estimate=pl.CostEstimate(flops=flops, bytes_accessed=5 * 2**20, transcendentals=0),
    )(*[pltpu.with_memory_space_constraint(x, pltpu.HBM) for x in operands])
    held = [pltpu.with_memory_space_constraint(x, pltpu.VMEM) for x in held]
    attn_out, grad_q, grad_k, grad_v = pl.pallas_call(
        store_kernel,
        out_shape=[jax.ShapeDtypeStruct(x.shape, BF16) for x in held],
        in_specs=[vmem_spec] * 4,
        out_specs=[any_spec] * 4,
        scratch_shapes=[dma((4,))],
        compiler_params=pltpu.CompilerParams(vmem_limit_bytes=16 * 2**20),
        cost_estimate=pl.CostEstimate(flops=0, bytes_accessed=5 * 2**20, transcendentals=0),
    )(*held)
    return attn_out.reshape(cotangent.shape), grad_q, grad_k, grad_v


def solution(mesh):
    in_specs = (
        P("dp", "tensor"),
        P("dp", "tensor"),
        P("dp", "tensor"),
        P(),
        P(),
        P(("dp", "tensor"), None),
        P(),
        P(),
        P(),
    )
    out_specs = (P(("dp", "tensor"), None), P("dp", "tensor"), P("dp", "tensor"), P("dp", "tensor"))
    return jax.shard_map(
        per_device, mesh=mesh, in_specs=in_specs, out_specs=out_specs, check_vma=False
    )
```
